32 devices in a mesh: dp: 16 (over z, y, core), mp: 2 (over x).
Axes of the slice: x: 2, y: 2, z: 4, core: 2. Of those that a mesh axis runs over, the one named last changes fastest.
Arguments:
- embed_in: bfloat16 [4096, 6144], P('dp', 'mp'), may hold values from -7.5 to 7.5
- block_grad: bfloat16 [4096, 6144], P('dp', 'mp'), may hold values from -6 to 6
- attn_grad: bfloat16 [4096, 6144], P('dp', 'mp'), may hold values from -5.7 to 5.7
- hidden_grad: bfloat16 [4096, 12288], P('dp', 'mp'), may hold values from -6 to 6
- up_weight: bfloat16 [6144, 12288], P('dp', 'mp'), may hold values from -0.078125 to 0.078125
- up_bias: float32 [12288], P('mp'), may hold values from -4 to 4
- norm_gain: float32 [6144], P('mp'), may hold values from 0.1 to 1.9
- patches: bfloat16 [4096, 588], P('dp'), may hold values from -5 to 5
Outputs:
- embed_grad: bfloat16 [4096, 6144], P('dp', 'mp')
- patch_weight_grad: float32 [588, 6144], P(None, 'mp')
The draws below stay inside these ranges and needn't reach their ends.
All inputs are finite; a program needn't handle non-finite values.
Results may differ from the reference program's by a relative error of at most 0.0046.
Values may be sent and summed in bfloat16 or wider, within the bound.
A program may use at most 192 MiB of HBM per device.

```python
import jax
import jax.numpy as jnp
from jax import lax

D = 6144
FF = 12288
P_SIZE = 588
IMAGES = 1
TOK = 256
TOKENS = 4096
N_DP = 16


def draw_embed_in(key, part):
    key = jax.random.fold_in(key, 5)
    noise_key, shift_key = jax.random.split(key)
    noise = jnp.clip(jax.random.normal(noise_key, (TOKENS, D), jnp.float32), -6.0, 6.0)
    shift = jax.random.uniform(shift_key, (TOKENS, 1), jnp.float32, -1.5, 1.5)
    return (noise + shift).astype(jnp.bfloat16)


def draw_attn_grad(key, part):
    key = jax.random.fold_in(key, 11)
    noise_key, shift_key = jax.random.split(key)
    noise = 0.7 * jnp.clip(jax.random.normal(noise_key, (TOKENS, D), jnp.float32), -6.0, 6.0)
    shift = jax.random.uniform(shift_key, (TOKENS, 1), jnp.float32, -1.5, 1.5)
    return (noise + shift).astype(jnp.bfloat16)


def with_spikes(entries, rng, source, target, parts, factor):
    def block_of(axis_at):
        return (jnp.arange(entries.shape[axis_at]) // (entries.shape[axis_at] // parts)).reshape((-1,) + (1,) * (entries.ndim - 1 - axis_at))

    one_side = jax.random.permutation(rng, parts)[block_of(target)]
    second = (block_of(target) + parts // 2) % parts
    return jnp.where((block_of(source) == one_side) | (block_of(source) == second), factor * entries, entries)


def level_of(stream_key, shape, shards, least, largest):
    def one(dim, parts):
        steps = jax.random.uniform(jax.random.fold_in(jax.random.fold_in(stream_key, 6), dim), (parts,), jnp.float32, least / len(shards), largest / len(shards))
        return jnp.repeat(jnp.exp(steps), shape[dim] // parts).reshape((-1,) + (1,) * (len(shape) - dim - 1))

    loudness = one(*shards[0])
    for cut in shards[1:]:
        loudness = loudness * one(*cut)
    return loudness


def normal_values(rng, extent, width, reach, pieces=(), kind=jnp.bfloat16):
    level = level_of(rng, extent, pieces, -0.22, 0.18) if pieces else 1.0
    array = jax.random.normal(rng, extent, jnp.float32) * width * level
    return jnp.minimum(jnp.maximum(array, -reach), reach).astype(kind)


def noise_with(rng, shape, scale, most, cuts, heavy, dtype=jnp.bfloat16):
    drawn = scale * jax.random.normal(rng, shape, jnp.float32)
    if cuts:
        drawn = drawn * level_of(rng, shape, cuts, -0.22, 0.18)
    return jnp.clip(with_spikes(drawn, jax.random.fold_in(rng, 3), *heavy), -most, most).astype(dtype)


def setup_inputs(seed: int = 0) -> dict:
    splits = jax.random.split(jax.random.key(seed), 9)
    embed_in = draw_embed_in(jax.random.fold_in(splits[8], 71), 0)
    block_grad = normal_values(splits[1], (TOKENS, D), 1.0, 6.0, ((0, 16), (1, 2)))
    attn_grad = draw_attn_grad(jax.random.fold_in(splits[8], 71), 0)
    hidden_grad = noise_with(splits[3], (TOKENS, FF), 1.0, 6.0, ((0, 16), (1, 2)), (1, 0, 16, 2.0))
    up_weight = normal_values(splits[4], (D, FF), D ** -0.5, 0.078125, ((0, 16), (1, 2)))
    up_bias = normal_values(splits[5], (FF,), 1.0, 4.0, ((0, 2),), jnp.float32)
    norm_gain = jnp.clip(1.0 + 0.18 * jax.random.normal(splits[6], (D,), jnp.float32), 0.1, 1.9)
    patches = normal_values(splits[7], (TOKENS, P_SIZE), 1.0, 5.0, ((0, 16),))
    return {"embed_in": embed_in, "block_grad": block_grad, "attn_grad": attn_grad, "hidden_grad": hidden_grad, "up_weight": up_weight, "up_bias": up_bias, "norm_gain": norm_gain, "patches": patches}


def gelu_slope(values):
    cdf_part = 0.5 * (1.0 + jax.scipy.special.erf(values * 0.7071067811865476))
    density = jnp.exp(-0.5 * values * values) * 0.3989422804014327
    return cdf_part + values * density

def reference(embed_in, block_grad, attn_grad, hidden_grad, up_weight, up_bias, norm_gain, patches):
    features = embed_in.astype(jnp.float32)
    centred = features - lax.optimization_barrier(jnp.mean(features, axis=-1, keepdims=True))
    inv_std = lax.rsqrt(lax.optimization_barrier(jnp.mean(centred * centred, axis=-1, keepdims=True)) + 1e-06)
    unit = centred * inv_std
    gain = norm_gain.astype(jnp.float32)
    normed = (unit * gain).astype(jnp.bfloat16)
    preact = jnp.dot(normed, up_weight, preferred_element_type=jnp.float32) + up_bias.astype(jnp.float32)
    delta = (hidden_grad.astype(jnp.float32) * gelu_slope(preact)).astype(jnp.bfloat16)
    branch = lax.dot_general(delta, up_weight, (((1,), (1,)), ((), ())), preferred_element_type=jnp.float32)
    branch = branch + attn_grad.astype(jnp.float32)
    scaled = branch * gain
    norm_back = inv_std * (scaled - lax.optimization_barrier(jnp.mean(scaled, axis=-1, keepdims=True)) - unit * lax.optimization_barrier(jnp.mean(scaled * unit, axis=-1, keepdims=True)))
    embed_grad = (block_grad.astype(jnp.float32) + norm_back).astype(jnp.bfloat16)
    grouped = embed_grad.reshape(N_DP, TOK, D).astype(jnp.float32)
    pixels = patches.reshape(N_DP, TOK, P_SIZE).astype(jnp.float32)
    summed = jnp.einsum('gtp,gtd->pd', pixels, grouped)
    patch_weight_grad = summed / (IMAGES * N_DP)
    return (embed_grad, patch_weight_grad)
```

```python
import math

import jax
import jax.numpy as jnp
from jax import lax
from jax.experimental import pallas as pl
from jax.sharding import PartitionSpec as P

D = 6144
IMAGES = 1
PIECES = 2


def gelu_slope(values):
    cdf_part = 0.5 * (1.0 + lax.erf(values * 0.7071067811865476))
    density = jnp.exp(-0.5 * values * values) * 0.3989422804014327
    return cdf_part + values * density


def swap(value):
    return lax.ppermute(value, "mp", [(0, 1), (1, 0)])


def gather_features(value, groups):
    if groups != 2:
        return lax.all_gather(value, "mp", axis=value.ndim - 1, tiled=True)
    other = swap(value)
    first = lax.axis_index("mp") == 0
    return jnp.concatenate([jnp.where(first, value, other), jnp.where(first, other, value)], -1)


def spread(part, name):
    count, width, rows = part.shape
    group = 128 // math.gcd(width, 128)

    def kernel(blocks_ref, out_ref):
        blocks = blocks_ref[...].astype(jnp.float32).reshape(group * width, rows)
        out_ref[...] = blocks.T

    return pl.pallas_call(
        kernel,
        grid=(count // group,),
        in_specs=[pl.BlockSpec((group, width, rows), lambda i: (i, 0, 0))],
        out_specs=pl.BlockSpec((rows, group * width), lambda i: (0, i)),
        out_shape=jax.ShapeDtypeStruct((rows, count * width), jnp.float32),
        name=name,
    )(part)


def tokens_product(left, right):
    return lax.dot_general(
        left, right, (((0,), (0,)), ((), ())), preferred_element_type=jnp.float32
    )


def patch_grad(patches_all, embed_grad):
    n = lax.axis_size("dp")
    factor = 1.0 / (n * IMAGES)
    columns = embed_grad.shape[1] // n
    mine = embed_grad.reshape(-1, n, columns).transpose(1, 0, 2)
    mine = lax.all_to_all(mine, "dp", 0, 0)
    part = tokens_product(mine.reshape(-1, columns), patches_all) * factor
    return spread(lax.all_gather(part.astype(jnp.bfloat16), "dp", axis=0), "spread_columns")


def branch_sum(delta, weight, normed, gain_all, groups):
    transposed = (((1,), (1,)), ((), ()))
    if groups != 2:
        terms = lax.dot_general(delta, weight, transposed, preferred_element_type=jnp.float32)
        own = lax.psum_scatter(terms, "mp", scatter_dimension=1, tiled=True)
        scaled = (terms * gain_all).sum(-1, keepdims=True)
        return own, scaled, (terms * normed.astype(jnp.float32)).sum(-1, keepdims=True)
    half = weight.shape[0] // 2
    width = half // PIECES
    first = lax.axis_index("mp") == 0
    own, scaled, paired = [], 0.0, 0.0
    for piece in range(PIECES):
        sides = []
        for start in (piece * width, half + piece * width):
            rows = slice(start, start + width)
            term = lax.dot_general(
                delta, weight[rows], transposed, preferred_element_type=jnp.float32
            )
            scaled += (term * gain_all[rows]).sum(-1, keepdims=True)
            paired += (term * normed[:, rows].astype(jnp.float32)).sum(-1, keepdims=True)
            sides.append(term)
        arrived = swap(jnp.where(first, sides[1], sides[0]).astype(jnp.bfloat16))
        own.append(jnp.where(first, sides[0], sides[1]) + arrived.astype(jnp.float32))
    return jnp.concatenate(own, axis=1), scaled, paired


def body(embed_in, block_grad, attn_grad, hidden_grad, up_weight, up_bias, norm_gain, patches):
    groups = lax.axis_size("mp")
    weight = lax.all_gather(up_weight, "dp", axis=0, tiled=True)
    patches_all = lax.all_gather(patches, "dp", axis=0, tiled=True)
    gain_all = gather_features(norm_gain, groups)
    features = embed_in.astype(jnp.float32)
    row_total, row_square = lax.psum(
        (
            jnp.sum(features, axis=-1, keepdims=True),
            jnp.sum(features * features, axis=-1, keepdims=True),
        ),
        "mp",
    )
    row_mean = row_total / D
    centred = features - row_mean
    variance = jnp.maximum(row_square / D - row_mean * row_mean, 0.0)
    inv_std = lax.rsqrt(variance + 1e-06)
    unit = centred * inv_std
    normed = gather_features((unit * norm_gain).astype(jnp.bfloat16), groups)
    normed, gain_all = lax.optimization_barrier((normed, gain_all))
    preact = jnp.dot(normed, weight, preferred_element_type=jnp.float32) + up_bias
    delta = (hidden_grad.astype(jnp.float32) * gelu_slope(preact)).astype(jnp.bfloat16)
    own_sum, scaled_share, paired_share = branch_sum(delta, weight, normed, gain_all, groups)
    attn = attn_grad.astype(jnp.float32)
    attn_scaled = attn * norm_gain
    scaled_total, paired_total = lax.psum(
        (
            scaled_share + jnp.sum(attn_scaled, axis=-1, keepdims=True),
            paired_share + jnp.sum(attn_scaled * unit, axis=-1, keepdims=True),
        ),
        "mp",
    )
    scaled = (own_sum + attn) * norm_gain
    norm_back = inv_std * (scaled - scaled_total / D - unit * (paired_total / D))
    embed_grad = (block_grad.astype(jnp.float32) + norm_back).astype(jnp.bfloat16)
    return (embed_grad, patch_grad(patches_all, embed_grad))


def solution(mesh):
    in_specs = (
        P("dp", "mp"),
        P("dp", "mp"),
        P("dp", "mp"),
        P("dp", "mp"),
        P("dp", "mp"),
        P("mp"),
        P("mp"),
        P("dp", None),
    )
    out_specs = (P("dp", "mp"), P(None, "mp"))
    return jax.shard_map(body, mesh=mesh, in_specs=in_specs, out_specs=out_specs, check_vma=False)
```

```python
import math

import jax
import jax.numpy as jnp
from jax import lax
from jax.experimental import pallas as pl
from jax.sharding import PartitionSpec as P

D = 6144
IMAGES = 1
PIECES = 4


def gelu_slope(values):
    cdf_part = 0.5 * (1.0 + lax.erf(values * 0.7071067811865476))
    density = jnp.exp(-0.5 * values * values) * 0.3989422804014327
    return cdf_part + values * density


def swap(value):
    return lax.ppermute(value, "mp", [(0, 1), (1, 0)])


def gather_features(value, groups):
    if groups != 2:
        return lax.all_gather(value, "mp", axis=value.ndim - 1, tiled=True)
    other = swap(value)
    first = lax.axis_index("mp") == 0
    return jnp.concatenate([jnp.where(first, value, other), jnp.where(first, other, value)], -1)


def spread(part, name):
    count, width, rows = part.shape
    group = 128 // math.gcd(width, 128)

    def kernel(blocks_ref, out_ref):
        blocks = blocks_ref[...].astype(jnp.float32).reshape(group * width, rows)
        out_ref[...] = blocks.T

    return pl.pallas_call(
        kernel,
        grid=(count // group,),
        in_specs=[pl.BlockSpec((group, width, rows), lambda i: (i, 0, 0))],
        out_specs=pl.BlockSpec((rows, group * width), lambda i: (0, i)),
        out_shape=jax.ShapeDtypeStruct((rows, count * width), jnp.float32),
        name=name,
    )(part)


def tokens_product(left, right):
    return lax.dot_general(
        left, right, (((0,), (0,)), ((), ())), preferred_element_type=jnp.float32
    )


def patch_grad(patches_all, embed_grad):
    n = lax.axis_size("dp")
    factor = 1.0 / (n * IMAGES)
    columns = embed_grad.shape[1] // n
    mine = embed_grad.reshape(-1, n, columns).transpose(1, 0, 2)
    mine = lax.all_to_all(mine, "dp", 0, 0)
    part = tokens_product(mine.reshape(-1, columns), patches_all) * factor
    return spread(lax.all_gather(part.astype(jnp.bfloat16), "dp", axis=0), "spread_columns")


def branch_sum(delta, weight, normed, gain_all, groups):
    transposed = (((1,), (1,)), ((), ()))
    if groups != 2:
        terms = lax.dot_general(delta, weight, transposed, preferred_element_type=jnp.float32)
        own = lax.psum_scatter(terms, "mp", scatter_dimension=1, tiled=True)
        scaled = (terms * gain_all).sum(-1, keepdims=True)
        return own, scaled, (terms * normed.astype(jnp.float32)).sum(-1, keepdims=True)
    half = weight.shape[0] // 2
    width = half // PIECES
    first = lax.axis_index("mp") == 0
    own, scaled, paired = [], 0.0, 0.0
    for piece in range(PIECES):
        sides = []
        for start in (piece * width, half + piece * width):
            rows = slice(start, start + width)
            term = lax.dot_general(
                delta, weight[rows], transposed, preferred_element_type=jnp.float32
            )
            scaled += (term * gain_all[rows]).sum(-1, keepdims=True)
            paired += (term * normed[:, rows].astype(jnp.float32)).sum(-1, keepdims=True)
            sides.append(term)
        arrived = swap(jnp.where(first, sides[1], sides[0]).astype(jnp.bfloat16))
        own.append(jnp.where(first, sides[0], sides[1]) + arrived.astype(jnp.float32))
    return jnp.concatenate(own, axis=1), scaled, paired


def body(embed_in, block_grad, attn_grad, hidden_grad, up_weight, up_bias, norm_gain, patches):
    groups = lax.axis_size("mp")
    weight = lax.all_gather(up_weight, "dp", axis=0, tiled=True)
    patches_all = lax.all_gather(patches, "dp", axis=0, tiled=True)
    gain_all = gather_features(norm_gain, groups)
    features = embed_in.astype(jnp.float32)
    row_total, row_square = lax.psum(
        (
            jnp.sum(features, axis=-1, keepdims=True),
            jnp.sum(features * features, axis=-1, keepdims=True),
        ),
        "mp",
    )
    row_mean = row_total / D
    centred = features - row_mean
    variance = jnp.maximum(row_square / D - row_mean * row_mean, 0.0)
    inv_std = lax.rsqrt(variance + 1e-06)
    unit = centred * inv_std
    normed = gather_features((unit * norm_gain).astype(jnp.bfloat16), groups)
    normed, gain_all = lax.optimization_barrier((normed, gain_all))
    preact = jnp.dot(normed, weight, preferred_element_type=jnp.float32) + up_bias
    delta = (hidden_grad.astype(jnp.float32) * gelu_slope(preact)).astype(jnp.bfloat16)
    own_sum, scaled_share, paired_share = branch_sum(delta, weight, normed, gain_all, groups)
    attn = attn_grad.astype(jnp.float32)
    attn_scaled = attn * norm_gain
    shares = jnp.concatenate(
        [
            scaled_share + jnp.sum(attn_scaled, axis=-1, keepdims=True),
            paired_share + jnp.sum(attn_scaled * unit, axis=-1, keepdims=True),
        ],
        axis=1,
    )
    totals = shares + swap(shares) if groups == 2 else lax.psum(shares, "mp")
    scaled_total, paired_total = totals[:, :1], totals[:, 1:]
    scaled = (own_sum + attn) * norm_gain
    norm_back = inv_std * (scaled - scaled_total / D - unit * (paired_total / D))
    embed_grad = (block_grad.astype(jnp.float32) + norm_back).astype(jnp.bfloat16)
    return (embed_grad, patch_grad(patches_all, embed_grad))


def solution(mesh):
    in_specs = (
        P("dp", "mp"),
        P("dp", "mp"),
        P("dp", "mp"),
        P("dp", "mp"),
        P("dp", "mp"),
        P("mp"),
        P("mp"),
        P("dp", None),
    )
    out_specs = (P("dp", "mp"), P(None, "mp"))
    return jax.shard_map(body, mesh=mesh, in_specs=in_specs, out_specs=out_specs, check_vma=False)
```

```python
import math

import jax
import jax.numpy as jnp
from jax import lax
from jax.experimental import pallas as pl
from jax.sharding import PartitionSpec as P

D = 6144
IMAGES = 1
PIECES = 6


def gelu_slope(values):
    cdf_part = 0.5 * (1.0 + lax.erf(values * 0.7071067811865476))
    density = jnp.exp(-0.5 * values * values) * 0.3989422804014327
    return cdf_part + values * density


def swap(value):
    return lax.ppermute(value, "mp", [(0, 1), (1, 0)])


def gather_features(value, groups):
    if groups != 2:
        return lax.all_gather(value, "mp", axis=value.ndim - 1, tiled=True)
    other = swap(value)
    first = lax.axis_index("mp") == 0
    return jnp.concatenate([jnp.where(first, value, other), jnp.where(first, other, value)], -1)


def spread(part, name):
    count, width, rows = part.shape
    group = 128 // math.gcd(width, 128)

    def kernel(blocks_ref, out_ref):
        blocks = blocks_ref[...].astype(jnp.float32).reshape(group * width, rows)
        out_ref[...] = blocks.T

    return pl.pallas_call(
        kernel,
        grid=(count // group,),
        in_specs=[pl.BlockSpec((group, width, rows), lambda i: (i, 0, 0))],
        out_specs=pl.BlockSpec((rows, group * width), lambda i: (0, i)),
        out_shape=jax.ShapeDtypeStruct((rows, count * width), jnp.float32),
        name=name,
    )(part)


def tokens_product(left, right):
    return lax.dot_general(
        left, right, (((0,), (0,)), ((), ())), preferred_element_type=jnp.float32
    )


def patch_grad(patches_all, embed_grad):
    n = lax.axis_size("dp")
    factor = 1.0 / (n * IMAGES)
    columns = embed_grad.shape[1] // n
    mine = embed_grad.reshape(-1, n, columns).transpose(1, 0, 2)
    mine = lax.all_to_all(mine, "dp", 0, 0)
    part = tokens_product(mine.reshape(-1, columns), patches_all) * factor
    return spread(lax.all_gather(part.astype(jnp.bfloat16), "dp", axis=0), "spread_columns")


def branch_sum(delta, weight, normed, gain_all, groups):
    transposed = (((1,), (1,)), ((), ()))
    if groups != 2:
        terms = lax.dot_general(delta, weight, transposed, preferred_element_type=jnp.float32)
        own = lax.psum_scatter(terms, "mp", scatter_dimension=1, tiled=True)
        scaled = (terms * gain_all).sum(-1, keepdims=True)
        return own, scaled, (terms * normed.astype(jnp.float32)).sum(-1, keepdims=True)
    half = weight.shape[0] // 2
    width = half // PIECES
    first = lax.axis_index("mp") == 0
    own, scaled, paired = [], 0.0, 0.0
    for piece in range(PIECES):
        sides = []
        for start in (piece * width, half + piece * width):
            rows = slice(start, start + width)
            term = lax.dot_general(
                delta, weight[rows], transposed, preferred_element_type=jnp.float32
            )
            scaled += (term * gain_all[rows]).sum(-1, keepdims=True)
            paired += (term * normed[:, rows].astype(jnp.float32)).sum(-1, keepdims=True)
            sides.append(term)
        arrived = swap(jnp.where(first, sides[1], sides[0]).astype(jnp.bfloat16))
        own.append(jnp.where(first, sides[0], sides[1]) + arrived.astype(jnp.float32))
    return jnp.concatenate(own, axis=1), scaled, paired


def body(embed_in, block_grad, attn_grad, hidden_grad, up_weight, up_bias, norm_gain, patches):
    groups = lax.axis_size("mp")
    weight = lax.all_gather(up_weight, "dp", axis=0, tiled=True)
    patches_all = lax.all_gather(patches, "dp", axis=0, tiled=True)
    gain_all = gather_features(norm_gain, groups)
    features = embed_in.astype(jnp.float32)
    row_total, row_square = lax.psum(
        (
            jnp.sum(features, axis=-1, keepdims=True),
            jnp.sum(features * features, axis=-1, keepdims=True),
        ),
        "mp",
    )
    row_mean = row_total / D
    centred = features - row_mean
    variance = jnp.maximum(row_square / D - row_mean * row_mean, 0.0)
    inv_std = lax.rsqrt(variance + 1e-06)
    unit = centred * inv_std
    normed = gather_features((unit * norm_gain).astype(jnp.bfloat16), groups)
    normed, gain_all = lax.optimization_barrier((normed, gain_all))
    preact = jnp.dot(normed, weight, preferred_element_type=jnp.float32) + up_bias
    delta = (hidden_grad.astype(jnp.float32) * gelu_slope(preact)).astype(jnp.bfloat16)
    own_sum, scaled_share, paired_share = branch_sum(delta, weight, normed, gain_all, groups)
    attn = attn_grad.astype(jnp.float32)
    attn_scaled = attn * norm_gain
    shares = jnp.concatenate(
        [
            scaled_share + jnp.sum(attn_scaled, axis=-1, keepdims=True),
            paired_share + jnp.sum(attn_scaled * unit, axis=-1, keepdims=True),
        ],
        axis=1,
    )
    totals = shares + swap(shares) if groups == 2 else lax.psum(shares, "mp")
    scaled_total, paired_total = totals[:, :1], totals[:, 1:]
    scaled = (own_sum + attn) * norm_gain
    norm_back = inv_std * (scaled - scaled_total / D - unit * (paired_total / D))
    embed_grad = (block_grad.astype(jnp.float32) + norm_back).astype(jnp.bfloat16)
    return (embed_grad, patch_grad(patches_all, embed_grad))


def solution(mesh):
    in_specs = (
        P("dp", "mp"),
        P("dp", "mp"),
        P("dp", "mp"),
        P("dp", "mp"),
        P("dp", "mp"),
        P("mp"),
        P("mp"),
        P("dp", None),
    )
    out_specs = (P("dp", "mp"), P(None, "mp"))
    return jax.shard_map(body, mesh=mesh, in_specs=in_specs, out_specs=out_specs, check_vma=False)
```
